32 devices in a mesh: groups: 2 (over y), tensor: 4 (over z), adapter: 2 (over x), sub: 2 (over core).
Axes of the slice: x: 2, y: 2, z: 4, core: 2. Of those that a mesh axis runs over, the one named last changes fastest.
Arguments:
- hidden: bfloat16 [1024, 2, 8192], P(('groups', 'tensor')), parts along dimension 0, may hold values from -6 to 6
- output_weight: bfloat16 [8192, 8192], P('tensor', ('adapter', 'sub')), may hold values from -0.0625 to 0.0625
- adapter_down_weight: bfloat16 [8192, 4096], P(('adapter', 'sub'), 'tensor'), may hold values from -0.0625 to 0.0625
- adapter_up_weight: bfloat16 [4096, 8192], P('tensor', ('adapter', 'sub')), may hold values from -0.75 to 0.75
- adapter_storage_slot: int32 [128], P('groups'), parts along dimension 0, may hold values from 0 to 63, as said below
- request_adapter: int32 [1024], P('groups'), parts along dimension 0, may hold values from 0 to 63, as said below
Outputs:
- projected: bfloat16 [1024, 2, 8192], P(('groups', 'tensor'), None, ('adapter', 'sub')), parts along dimension 0
The draws below stay inside these ranges and needn't reach their ends.
There are 2 independent parts, one for each index of `groups`. The reference program is written for one: setup_inputs(seed, part) draws one part's arguments, and reference() takes and returns one part's arrays. A program takes and returns all parts, laid end to end along the dimension named above; an argument that names none is the same for every part. Nothing has to cross between parts.
Inputs may be any that keep to these rules, and one draw needn't show every extreme that they name: `adapter_storage_slot`: each storage slot is taken by exactly one adapter. Holder of a row: adapter_storage_slot[request_adapter[r]] // 16. In each aligned block of 128 rows, at most 64 rows have the same holder, and in every draw one holder has exactly 64 rows in every block.
All inputs are finite; a program needn't handle non-finite values.
Results may differ from the reference program's by a relative error of at most 0.0085.
Values may be sent and summed in bfloat16 or wider, within the bound.
A program may use at most 192 MiB of HBM per device.

```python
import jax
import jax.numpy as jnp
from jax import lax

MODEL_WIDTH = 8192
ADAPTER_RANK = 64
ADP_HOLD = 16
STEPS = 2
ROW_DEV = 128
ADAPTER_COUNT = 64
ROWS = 512
HOLDERS = 4
CAP = 64
SLOTS = 256


def routing(key):
    placement = jax.random.permutation(jax.random.fold_in(key, 101), ADAPTER_COUNT).astype(jnp.int32)
    hot_holder = jax.random.randint(jax.random.fold_in(key, 102), (), 0, HOLDERS)
    sources = ROWS // ROW_DEV
    slot_index = jnp.arange(SLOTS, dtype=jnp.int32)
    scores = jax.random.randint(jax.random.fold_in(key, 103), (sources, SLOTS), 0, 2 ** 20) * SLOTS + slot_index[None, :]
    scores = scores - jnp.where(slot_index[None, :] // CAP == hot_holder, 2 ** 29, 0)
    ordered = jnp.argsort(scores, axis=1)[:, :ROW_DEV]
    mixing = jax.random.randint(jax.random.fold_in(key, 104), (sources, ROW_DEV), 0, 2 ** 20) * ROW_DEV + jnp.arange(ROW_DEV, dtype=jnp.int32)[None, :]
    shuffle = jnp.argsort(mixing, axis=1)
    chosen = jnp.take_along_axis(ordered, shuffle, axis=1)
    holder = chosen // CAP
    local_choice = jax.random.randint(jax.random.fold_in(key, 105), (sources, ROW_DEV), 0, ADP_HOLD)
    storage = holder * ADP_HOLD + local_choice
    inverse = jnp.zeros((ADAPTER_COUNT,), jnp.int32).at[placement].set(jnp.arange(ADAPTER_COUNT, dtype=jnp.int32))
    identities = inverse[storage.reshape(ROWS)]
    return (placement, identities.astype(jnp.int32))


def draw_adapter_storage_slot(key, part):
    placement, identities = routing(key)
    return placement


def draw_request_adapter(key, part):
    placement, identities = routing(key)
    return identities


def levels(stream_key, extent, cuts, least, top_value):
    def one(dim, blocks):
        draws = jax.random.uniform(jax.random.fold_in(jax.random.fold_in(stream_key, 6), dim), (blocks,), jnp.float32, least / len(cuts), top_value / len(cuts))
        return jnp.repeat(jnp.exp(draws), extent[dim] // blocks).reshape((-1,) + (1,) * (len(extent) - dim - 1))

    gain = one(*cuts[0])
    for cut in cuts[1:]:
        gain = gain * one(*cut)
    return gain


def noise(own_key, shape, spread, reach, split=(), kind=jnp.bfloat16):
    factor_of = levels(own_key, shape, split, -0.22, 0.18) if split else 1.0
    result = jax.random.normal(own_key, shape, jnp.float32) * spread * factor_of
    return jnp.minimum(jnp.maximum(result, -reach), reach).astype(kind)


def setup_inputs(seed: int = 0, part: int = 0) -> dict:
    streams_of = jax.random.split(jax.random.key(seed), 7)
    part_keys = jax.random.split(jax.random.fold_in(streams_of[6], part), 7)
    hidden = noise(part_keys[0], (ROWS, STEPS, MODEL_WIDTH), 1.0, 6.0, ((0, 4),))
    output_weight = noise(streams_of[1], (MODEL_WIDTH, MODEL_WIDTH), MODEL_WIDTH ** -0.5, 0.0625, ((0, 4), (1, 4)))
    adapter_down_weight = noise(streams_of[2], (MODEL_WIDTH, ADAPTER_COUNT * ADAPTER_RANK), MODEL_WIDTH ** -0.5, 0.0625, ((0, 4), (1, 4)))
    adapter_up_weight = noise(streams_of[3], (ADAPTER_COUNT * ADAPTER_RANK, MODEL_WIDTH), ADAPTER_RANK ** -0.5, 0.75, ((0, 4), (1, 4)))
    adapter_storage_slot = draw_adapter_storage_slot(jax.random.fold_in(jax.random.fold_in(streams_of[6], part), 71), part)
    request_adapter = draw_request_adapter(jax.random.fold_in(jax.random.fold_in(streams_of[6], part), 71), part)
    return {"hidden": hidden, "output_weight": output_weight, "adapter_down_weight": adapter_down_weight, "adapter_up_weight": adapter_up_weight, "adapter_storage_slot": adapter_storage_slot, "request_adapter": request_adapter}


ADAPTER_SCALE = 0.5


def reference(hidden, output_weight, adapter_down_weight, adapter_up_weight, adapter_storage_slot, request_adapter):
    flat_rows = hidden.reshape(ROWS * STEPS, MODEL_WIDTH)
    shard_width = MODEL_WIDTH // HOLDERS
    base_output_sum = jnp.zeros((ROWS * STEPS, MODEL_WIDTH), jnp.float32)
    for column_block in range(HOLDERS):
        lower = column_block * shard_width
        partial_value = jnp.dot(flat_rows[:, lower:lower + shard_width], output_weight[lower:lower + shard_width, :], preferred_element_type=jnp.float32)
        base_output_sum = base_output_sum + lax.optimization_barrier(partial_value.astype(jnp.bfloat16)).astype(jnp.float32)
    slot = adapter_storage_slot[request_adapter].astype(jnp.int32)
    row_slots = jnp.repeat(slot, STEPS).astype(jnp.int32)
    down_weight_table = adapter_down_weight.reshape(MODEL_WIDTH, ADAPTER_COUNT, ADAPTER_RANK)
    up_weight_table = adapter_up_weight.reshape(ADAPTER_COUNT, ADAPTER_RANK, MODEL_WIDTH)

    def one_block(operands):
        row_block, slot_block = operands
        down_rows = jnp.take(down_weight_table, slot_block, axis=1)
        rank_partial_sum = jnp.einsum("rk,krq->rq", row_block.astype(jnp.float32), down_rows.astype(jnp.float32))
        rank_start_index = (ADAPTER_SCALE * rank_partial_sum).astype(jnp.bfloat16)
        up_weight_rows = jnp.take(up_weight_table, slot_block, axis=0)
        adapter_delta = jnp.einsum("sk,skp->sp", rank_start_index.astype(jnp.float32), up_weight_rows.astype(jnp.float32))
        return adapter_delta.astype(jnp.bfloat16)

    deltas = lax.map(one_block, (flat_rows.reshape(-1, 16, MODEL_WIDTH), row_slots.reshape(-1, 16)))
    projected = base_output_sum + deltas.reshape(ROWS * STEPS, MODEL_WIDTH).astype(jnp.float32)
    return projected.astype(jnp.bfloat16).reshape(ROWS, STEPS, MODEL_WIDTH)
```

```python
import functools

import jax
import jax.numpy as jnp
from jax import lax
from jax.experimental import pallas as pl
from jax.experimental.pallas import tpu as pltpu
from jax.sharding import PartitionSpec as P

ADAPTER_RANK = 64
ADP_HOLD = 16
ADAPTER_SCALE = 0.5
CHUNKS = 2
LANES = 128
MESH = pl.DeviceIdType.MESH


def kernel(
    T, A, S, C,
    hq_in, ht_in, w_in, down_in, up_in, code_ref, out_ref,
    hq, ht, w, down, up, z, spread, acc, part, rb,
    load_sem, loc_sem, ag_send, ag_recv, bc_send, bc_recv, z_send, z_recv, rs_send, rs_recv,
):
    Q = A * S
    t = lax.axis_index("tensor")
    a = lax.axis_index("adapter")
    s = lax.axis_index("sub")
    q = a * S + s
    rows = hq.shape[1]
    M = rows // C
    N = w.shape[1]
    X = down.shape[1]
    root_a, root_s = t // S, t % S
    is_root = q == t
    in_column = s == root_s

    def chunk(c):
        return pl.ds(c * M, M)

    def when(cond):
        return pl.when(cond)

    loads = [
        pltpu.make_async_copy(hq_in, hq.at[t], load_sem.at[0]),
        pltpu.make_async_copy(down_in, down, load_sem.at[1]),
        pltpu.make_async_copy(ht_in, ht.at[t], load_sem.at[2]),
        pltpu.make_async_copy(w_in, w, load_sem.at[3]),
        pltpu.make_async_copy(up_in, up, load_sem.at[4]),
    ]
    for copy in loads:
        copy.start()

    barrier = pltpu.get_barrier_semaphore()

    @when(t > 0)
    def _():
        pl.semaphore_signal(barrier, inc=1, device_id={"tensor": t - 1}, device_id_type=MESH)

    @when(t < T - 1)
    def _():
        pl.semaphore_signal(barrier, inc=1, device_id={"tensor": t + 1}, device_id_type=MESH)

    for off in range(1, Q):
        peer = lax.rem(q + off, Q)
        pl.semaphore_signal(
            barrier, inc=1, device_id={"adapter": peer // S, "sub": peer % S}, device_id_type=MESH
        )
    pl.semaphore_wait(barrier, Q - 1 + (t + T - 1) // T + (T - 1 - t + T - 1) // T)

    def gather_copy(d, c, side, own=False):
        source = hq_in.at[chunk(c), :] if own else hq.at[d, chunk(c), :]
        return pltpu.make_async_remote_copy(
            src_ref=source,
            dst_ref=hq.at[d, chunk(c), :],
            send_sem=ag_send.at[side, d, c],
            recv_sem=ag_recv.at[d, c],
            device_id={"tensor": t + 1 if side else t - 1},
            device_id_type=MESH,
        )

    def gather_send(d, c, side, own=False):
        @when((t < T - 1) if side else (t > 0))
        def _():
            gather_copy(d, c, side, own).start()

    def spread_copy(d, c, k, source, target):
        return pltpu.make_async_remote_copy(
            src_ref=source.at[d, chunk(c), :],
            dst_ref=ht.at[d, chunk(c), :],
            send_sem=bc_send.at[k, d, c],
            recv_sem=bc_recv.at[d, c],
            device_id=target,
            device_id_type=MESH,
        )

    def column_target(k):
        return {"adapter": lax.rem(a + k, A)}

    def sibling_target(k):
        return {"sub": lax.rem(s + k, S)}

    def local_copy(d, c):
        return pltpu.make_async_copy(
            hq.at[d, chunk(c), :], ht.at[d, chunk(c), :], loc_sem.at[d, c]
        )

    def rank_copy(d, c, off):
        peer = lax.rem(q + off, Q)
        return pltpu.make_async_remote_copy(
            src_ref=z.at[q, d, chunk(c), :],
            dst_ref=z.at[q, d, chunk(c), :],
            send_sem=z_send.at[off, d, c],
            recv_sem=z_recv.at[q, d, c],
            device_id={"adapter": peer // S, "sub": peer % S},
            device_id_type=MESH,
        )

    def rank_wait(d, c, off):
        peer = lax.rem(q + off, Q)
        pltpu.make_async_remote_copy(
            src_ref=z.at[peer, d, chunk(c), :],
            dst_ref=z.at[peer, d, chunk(c), :],
            send_sem=z_send.at[off, d, c],
            recv_sem=z_recv.at[peer, d, c],
            device_id={"adapter": peer // S, "sub": peer % S},
            device_id_type=MESH,
        ).wait_recv()

    def low_rank(d, c):
        code = code_ref[d, chunk(c), :]
        value = hq[d, chunk(c), :]
        total = jnp.zeros((M, LANES), jnp.float32)
        wide = 256
        for j in range(X // wide):
            product = jnp.dot(
                value, down[:, j * wide:(j + 1) * wide], preferred_element_type=jnp.float32
            )
            holder = (lax.broadcasted_iota(jnp.int32, (M, wide), 1) + j * wide) // ADAPTER_RANK
            product = jnp.where(holder == code, product, 0.0)
            for k in range(wide // LANES):
                total = total + product[:, k * LANES:(k + 1) * LANES]
        z[q, d, chunk(c), :] = total.astype(jnp.bfloat16)

        @pl.loop(1, Q)
        def _(off):
            rank_copy(d, c, off).start()

    def base(d, c):
        tile = min(N, 512)

        @pl.loop(0, N // tile)
        def _(j):
            cols = pl.ds(pl.multiple_of(j * tile, tile), tile)
            acc[:, cols] = jnp.dot(
                ht[d, chunk(c), :], w[:, cols], preferred_element_type=jnp.float32
            )

    def finish(d, c):
        @pl.loop(1, Q)
        def _(off):
            rank_wait(d, c, off)

        low = jnp.zeros((M, LANES), jnp.float32)
        for k in range(Q):
            low = low + z[k, d, chunk(c), :].astype(jnp.float32)
        low = (low * ADAPTER_SCALE).astype(jnp.bfloat16)
        code = code_ref[d, chunk(c), :]
        for j in range(X // LANES):
            holder = (lax.broadcasted_iota(jnp.int32, (M, LANES), 1) + j * LANES) // ADAPTER_RANK
            spread[:, j * LANES:(j + 1) * LANES] = jnp.where(
                holder == code, low.astype(jnp.float32), 0.0
            ).astype(jnp.bfloat16)
        tile = min(N, 512)

        @pl.loop(0, N // tile)
        def _(j):
            cols = pl.ds(pl.multiple_of(j * tile, tile), tile)
            delta = jnp.dot(spread[...], up[:, cols], preferred_element_type=jnp.float32)
            part[d, chunk(c), cols] = (acc[:, cols] + delta).astype(jnp.bfloat16)

    def arrive(d, c, side):
        pltpu.make_async_remote_copy(
            src_ref=hq.at[d, chunk(c), :],
            dst_ref=hq.at[d, chunk(c), :],
            send_sem=ag_send.at[side, d, c],
            recv_sem=ag_recv.at[d, c],
            device_id={"tensor": lax.rem(t + 1, T)},
            device_id_type=MESH,
        ).wait_recv()
        gather_send(d, c, side)

        @when(is_root)
        def _():
            for k in range(1, A):
                spread_copy(d, c, k - 1, hq, column_target(k)).start()
            for k in range(1, S):
                spread_copy(d, c, A - 2 + k, hq, sibling_target(k)).start()
            local_copy(d, c).start()

    def features(d, c):
        @when(is_root)
        def _():
            local_copy(d, c).wait()

        @when(jnp.logical_not(is_root))
        def _():
            spread_copy(d, c, 0, ht, sibling_target(1)).wait_recv()

        @when(jnp.logical_and(in_column, jnp.logical_not(is_root)))
        def _():
            for k in range(1, S):
                spread_copy(d, c, A - 2 + k, ht, sibling_target(k)).start()

    def both_sides(dist, body):
        @when(t + dist < T)
        def _():
            body(t + dist, 0)

        @when(t - dist >= 0)
        def _():
            body(t - dist, 1)

    def gather_step(dist, c):
        both_sides(dist, lambda d, side: arrive(d, c, side))
        if isinstance(dist, int):
            pass
        both_sides(dist, lambda d, side: low_rank(d, c))

        def second(d, side):
            features(d, c)
            base(d, c)
            finish(d, c)

        both_sides(dist, second)

    def sum_copy(d, slot, c, side):
        return pltpu.make_async_remote_copy(
            src_ref=part.at[d, chunk(c), :],
            dst_ref=rb.at[slot, chunk(c), :],
            send_sem=rs_send.at[d, c],
            recv_sem=rs_recv.at[slot, c],
            device_id={"tensor": t + 1 if side else t - 1},
            device_id_type=MESH,
        )

    def sum_wait(slot, c):
        pltpu.make_async_remote_copy(
            src_ref=rb.at[slot, chunk(c), :],
            dst_ref=rb.at[slot, chunk(c), :],
            send_sem=rs_send.at[0, c],
            recv_sem=rs_recv.at[slot, c],
            device_id={"tensor": lax.rem(t + 1, T)},
            device_id_type=MESH,
        ).wait_recv()

    def add_arrived(d, c):
        sum_wait(d, c)
        part[d, chunk(c), :] = (
            part[d, chunk(c), :].astype(jnp.float32) + rb[d, chunk(c), :].astype(jnp.float32)
        ).astype(jnp.bfloat16)

    def sum_step(dist, c):
        @when(t + dist < T)
        def _():
            d = t + dist

            @when(t > 0)
            def _():
                add_arrived(d, c)

            sum_copy(d, d, c, 1).start()

        @when(t - dist >= 0)
        def _():
            d = t - dist

            @when(t < T - 1)
            def _():
                add_arrived(d, c)

            slot = jnp.where(dist == 1, T, d)
            sum_copy(d, slot, c, 0).start()

    def last(c):
        @when(t > 0)
        def _():
            sum_wait(t, c)

        @when(t < T - 1)
        def _():
            sum_wait(T, c)

        total = part[t, chunk(c), :].astype(jnp.float32)
        left = rb[t, chunk(c), :].astype(jnp.float32)
        right = rb[T, chunk(c), :].astype(jnp.float32)
        total = total + jnp.where(t > 0, left, 0.0) + jnp.where(t < T - 1, right, 0.0)
        out_ref[chunk(c), :] = total.astype(jnp.bfloat16)

    def own_sends(c):
        gather_send(t, c, 0, own=True)
        gather_send(t, c, 1, own=True)

    own_sends(0)
    loads[0].wait()
    loads[1].wait()
    for c in range(C):
        low_rank(t, c)
    loads[2].wait()
    loads[3].wait()
    loads[4].wait()
    for c in range(C):
        base(t, c)
        finish(t, c)

    for c in range(C):
        @pl.loop(1, T)
        def _(dist):
            if c > 0:
                sum_step(T - dist, c - 1)
            gather_step(dist, c)
            if c + 1 < C:
                @when(dist == 1)
                def _():
                    own_sends(c + 1)

        if c > 0:
            last(c - 1)

    @pl.loop(1, T)
    def _(dist):
        sum_step(T - dist, C - 1)

    last(C - 1)

    @pl.loop(0, T)
    def _(d):
        for c in range(C):
            @when(jnp.logical_and(d >= t, t > 0))
            def _():
                gather_copy(d, c, 0).wait_send()

            @when(jnp.logical_and(d <= t, t < T - 1))
            def _():
                gather_copy(d, c, 1).wait_send()

            @pl.loop(1, Q)
            def _(off):
                rank_copy(d, c, off).wait_send()

            @when(d != t)
            def _():
                sum_copy(d, d, c, 1).wait_send()

                @when(is_root)
                def _():
                    for k in range(1, A):
                        spread_copy(d, c, k - 1, hq, column_target(k)).wait_send()

                @when(in_column)
                def _():
                    for k in range(1, S):
                        spread_copy(d, c, A - 2 + k, ht, sibling_target(k)).wait_send()


def row_codes(adapter_storage_slot, request_adapter, steps):
    catalog = adapter_storage_slot.shape[0]
    matches = request_adapter[:, None] == jnp.arange(catalog, dtype=jnp.int32)[None, :]
    storage = jnp.sum(jnp.where(matches, adapter_storage_slot[None, :], 0), axis=1)
    local_slot = storage - lax.axis_index("tensor") * ADP_HOLD
    return jnp.repeat(local_slot, steps)


def local(
    hidden,
    output_weight,
    adapter_down_weight,
    adapter_up_weight,
    adapter_storage_slot,
    request_adapter,
):
    row_dev, steps, _ = hidden.shape
    T = lax.axis_size("tensor")
    A = lax.axis_size("adapter")
    S = lax.axis_size("sub")
    Q = A * S
    C = CHUNKS
    t = lax.axis_index("tensor")
    q = lax.axis_index(("adapter", "sub"))
    K, N = output_weight.shape
    KQ, X = adapter_down_weight.shape
    assert T == Q and K == KQ
    R = row_dev * steps
    hq = lax.dynamic_slice_in_dim(hidden, q * KQ, KQ, 2).reshape(R, KQ)
    ht = lax.dynamic_slice_in_dim(hidden, t * K, K, 2).reshape(R, K)
    codes = row_codes(adapter_storage_slot, request_adapter, steps).reshape(T, R, 1)
    bf = jnp.bfloat16
    dma = pltpu.SemaphoreType.DMA
    vmem = pl.BlockSpec(memory_space=pltpu.VMEM)
    anywhere = pl.BlockSpec(memory_space=pl.ANY)
    out = pl.pallas_call(
        functools.partial(kernel, T, A, S, C),
        out_shape=jax.ShapeDtypeStruct((R, N), bf),
        in_specs=[anywhere] * 5 + [vmem],
        out_specs=vmem,
        scratch_shapes=[
            pltpu.VMEM((T, R, KQ), bf),
            pltpu.VMEM((T, R, K), bf),
            pltpu.VMEM((K, N), bf),
            pltpu.VMEM((KQ, X), bf),
            pltpu.VMEM((X, N), bf),
            pltpu.VMEM((Q, T, R, LANES), bf),
            pltpu.VMEM((R // C, X), bf),
            pltpu.VMEM((R // C, N), jnp.float32),
            pltpu.VMEM((T, R, N), bf),
            pltpu.VMEM((T + 1, R, N), bf),
            dma((5,)),
            dma((T, C)),
            dma((2, T, C)),
            dma((T, C)),
            dma((A + S - 2, T, C)),
            dma((T, C)),
            dma((Q, T, C)),
            dma((Q, T, C)),
            dma((T, C)),
            dma((T + 1, C)),
        ],
        compiler_params=pltpu.CompilerParams(
            collective_id=0, has_side_effects=True, vmem_limit_bytes=56 * 1024 * 1024
        ),
        cost_estimate=pl.CostEstimate(
            flops=2 * T * R * (K * N + KQ * X + X * N),
            bytes_accessed=2 * (K * N + KQ * X + X * N + 4 * T * R * K),
            transcendentals=0,
        ),
    )(hq, ht, output_weight, adapter_down_weight, adapter_up_weight, codes)
    return out.reshape(row_dev, steps, N)


def solution(mesh):
    return jax.shard_map(
        local,
        mesh=mesh,
        in_specs=(
            P(("groups", "tensor"), None, None),
            P("tensor", ("adapter", "sub")),
            P(("adapter", "sub"), "tensor"),
            P("tensor", ("adapter", "sub")),
            P("groups"),
            P("groups"),
        ),
        out_specs=P(("groups", "tensor"), None, ("adapter", "sub")),
        check_vma=False,
    )
```

```python
import functools

import jax
import jax.numpy as jnp
from jax import lax
from jax.experimental import pallas as pl
from jax.experimental.pallas import tpu as pltpu
from jax.sharding import PartitionSpec as P

ADAPTER_RANK = 64
ADP_HOLD = 16
ADAPTER_SCALE = 0.5
CHUNKS = 2
LANES = 128
MESH = pl.DeviceIdType.MESH


def kernel(
    T, A, S, C,
    hq_in, ht_in, w_in, down_in, up_in, code_ref, out_ref,
    hq, ht, w, down, up, z, spread, acc, part, rb,
    load_sem, loc_sem, ag_send, ag_recv, bc_send, bc_recv, z_send, z_recv, rs_send, rs_recv,
):
    Q = A * S
    t = lax.axis_index("tensor")
    a = lax.axis_index("adapter")
    s = lax.axis_index("sub")
    q = a * S + s
    rows = hq.shape[1]
    M = rows // C
    N = w.shape[1]
    X = down.shape[1]
    root_a, root_s = t // S, t % S
    is_root = q == t
    in_column = s == root_s

    def chunk(c):
        return pl.ds(c * M, M)

    def when(cond):
        return pl.when(cond)

    loads = [
        pltpu.make_async_copy(hq_in, hq.at[t], load_sem.at[0]),
        pltpu.make_async_copy(down_in, down, load_sem.at[1]),
        pltpu.make_async_copy(ht_in, ht.at[t], load_sem.at[2]),
        pltpu.make_async_copy(w_in, w, load_sem.at[3]),
        pltpu.make_async_copy(up_in, up, load_sem.at[4]),
    ]
    for copy in loads:
        copy.start()

    barrier = pltpu.get_barrier_semaphore()

    @when(t > 0)
    def _():
        pl.semaphore_signal(barrier, inc=1, device_id={"tensor": t - 1}, device_id_type=MESH)

    @when(t < T - 1)
    def _():
        pl.semaphore_signal(barrier, inc=1, device_id={"tensor": t + 1}, device_id_type=MESH)

    for off in range(1, Q):
        peer = lax.rem(q + off, Q)
        pl.semaphore_signal(
            barrier, inc=1, device_id={"adapter": peer // S, "sub": peer % S}, device_id_type=MESH
        )
    pl.semaphore_wait(barrier, Q - 1 + (t + T - 1) // T + (T - 1 - t + T - 1) // T)

    def gather_copy(d, c, side, own=False):
        source = hq_in.at[chunk(c), :] if own else hq.at[d, chunk(c), :]
        return pltpu.make_async_remote_copy(
            src_ref=source,
            dst_ref=hq.at[d, chunk(c), :],
            send_sem=ag_send.at[side, d, c],
            recv_sem=ag_recv.at[d, c],
            device_id={"tensor": t + 1 if side else t - 1},
            device_id_type=MESH,
        )

    def gather_send(d, c, side, own=False):
        @when((t < T - 1) if side else (t > 0))
        def _():
            gather_copy(d, c, side, own).start()

    def spread_copy(d, c, k, source, target):
        return pltpu.make_async_remote_copy(
            src_ref=source.at[d, chunk(c), :],
            dst_ref=ht.at[d, chunk(c), :],
            send_sem=bc_send.at[k, d, c],
            recv_sem=bc_recv.at[d, c],
            device_id=target,
            device_id_type=MESH,
        )

    def column_target(k):
        return {"adapter": lax.rem(a + k, A)}

    def sibling_target(k):
        return {"sub": lax.rem(s + k, S)}

    def local_copy(d, c):
        return pltpu.make_async_copy(
            hq.at[d, chunk(c), :], ht.at[d, chunk(c), :], loc_sem.at[d, c]
        )

    def rank_copy(d, c, off):
        peer = lax.rem(q + off, Q)
        return pltpu.make_async_remote_copy(
            src_ref=z.at[q, d, chunk(c), :],
            dst_ref=z.at[q, d, chunk(c), :],
            send_sem=z_send.at[off, d, c],
            recv_sem=z_recv.at[q, d, c],
            device_id={"adapter": peer // S, "sub": peer % S},
            device_id_type=MESH,
        )

    def rank_wait(d, c, off):
        peer = lax.rem(q + off, Q)
        pltpu.make_async_remote_copy(
            src_ref=z.at[peer, d, chunk(c), :],
            dst_ref=z.at[peer, d, chunk(c), :],
            send_sem=z_send.at[off, d, c],
            recv_sem=z_recv.at[peer, d, c],
            device_id={"adapter": peer // S, "sub": peer % S},
            device_id_type=MESH,
        ).wait_recv()

    def lane_holder(first):
        return (lax.broadcasted_iota(jnp.int32, (M, LANES), 1) + first) // ADAPTER_RANK

    def low_rank(d, c):
        code = code_ref[d, chunk(c), :]
        value = hq[d, chunk(c), :]
        total = jnp.zeros((M, LANES), jnp.float32)
        wide = 256
        for j in range(X // wide):
            product = jnp.dot(
                value, down[:, j * wide:(j + 1) * wide], preferred_element_type=jnp.float32
            )
            for k in range(wide // LANES):
                holder = lane_holder(j * wide + k * LANES)
                total = total + jnp.where(
                    holder == code, product[:, k * LANES:(k + 1) * LANES], 0.0
                )
        z[q, d, chunk(c), :] = total.astype(jnp.bfloat16)

        @pl.loop(1, Q)
        def _(off):
            rank_copy(d, c, off).start()

    def base(d, c):
        tile = min(N, 512)

        @pl.loop(0, N // tile)
        def _(j):
            cols = pl.ds(pl.multiple_of(j * tile, tile), tile)
            acc[:, cols] = jnp.dot(
                ht[d, chunk(c), :], w[:, cols], preferred_element_type=jnp.float32
            )

    def finish(d, c):
        @pl.loop(1, Q)
        def _(off):
            rank_wait(d, c, off)

        low = jnp.zeros((M, LANES), jnp.float32)
        for k in range(Q):
            low = low + z[k, d, chunk(c), :].astype(jnp.float32)
        low = (low * ADAPTER_SCALE).astype(jnp.bfloat16)
        code = code_ref[d, chunk(c), :]
        for j in range(X // LANES):
            holder = lane_holder(j * LANES)
            spread[:, j * LANES:(j + 1) * LANES] = jnp.where(
                holder == code, low.astype(jnp.float32), 0.0
            ).astype(jnp.bfloat16)
        tile = min(N, 512)

        @pl.loop(0, N // tile)
        def _(j):
            cols = pl.ds(pl.multiple_of(j * tile, tile), tile)
            delta = jnp.dot(spread[...], up[:, cols], preferred_element_type=jnp.float32)
            part[d, chunk(c), cols] = (acc[:, cols] + delta).astype(jnp.bfloat16)

    def arrive(d, c, side):
        pltpu.make_async_remote_copy(
            src_ref=hq.at[d, chunk(c), :],
            dst_ref=hq.at[d, chunk(c), :],
            send_sem=ag_send.at[side, d, c],
            recv_sem=ag_recv.at[d, c],
            device_id={"tensor": lax.rem(t + 1, T)},
            device_id_type=MESH,
        ).wait_recv()
        gather_send(d, c, side)

        @when(is_root)
        def _():
            for k in range(1, A):
                spread_copy(d, c, k - 1, hq, column_target(k)).start()
            for k in range(1, S):
                spread_copy(d, c, A - 2 + k, hq, sibling_target(k)).start()
            local_copy(d, c).start()

    def features(d, c):
        @when(is_root)
        def _():
            local_copy(d, c).wait()

        @when(jnp.logical_not(is_root))
        def _():
            spread_copy(d, c, 0, ht, sibling_target(1)).wait_recv()

        @when(jnp.logical_and(in_column, jnp.logical_not(is_root)))
        def _():
            for k in range(1, S):
                spread_copy(d, c, A - 2 + k, ht, sibling_target(k)).start()

    def both_sides(dist, body):
        @when(t + dist < T)
        def _():
            body(t + dist, 0)

        @when(t - dist >= 0)
        def _():
            body(t - dist, 1)

    def gather_step(dist, c):
        both_sides(dist, lambda d, side: arrive(d, c, side))
        both_sides(dist, lambda d, side: low_rank(d, c))

    def feature_step(dist, c):
        both_sides(dist, lambda d, side: features(d, c))

    def project(d, c):
        base(d, c)
        finish(d, c)

    def project_step(dist, c):
        both_sides(dist, lambda d, side: project(d, c))

    def sum_copy(d, slot, c, side):
        return pltpu.make_async_remote_copy(
            src_ref=part.at[d, chunk(c), :],
            dst_ref=rb.at[slot, chunk(c), :],
            send_sem=rs_send.at[d, c],
            recv_sem=rs_recv.at[slot, c],
            device_id={"tensor": t + 1 if side else t - 1},
            device_id_type=MESH,
        )

    def sum_wait(slot, c):
        pltpu.make_async_remote_copy(
            src_ref=rb.at[slot, chunk(c), :],
            dst_ref=rb.at[slot, chunk(c), :],
            send_sem=rs_send.at[0, c],
            recv_sem=rs_recv.at[slot, c],
            device_id={"tensor": lax.rem(t + 1, T)},
            device_id_type=MESH,
        ).wait_recv()

    def add_arrived(d, c):
        sum_wait(d, c)
        part[d, chunk(c), :] = (
            part[d, chunk(c), :].astype(jnp.float32) + rb[d, chunk(c), :].astype(jnp.float32)
        ).astype(jnp.bfloat16)

    def sum_step(dist, c):
        @when(t + dist < T)
        def _():
            d = t + dist

            @when(t > 0)
            def _():
                add_arrived(d, c)

            sum_copy(d, d, c, 1).start()

        @when(t - dist >= 0)
        def _():
            d = t - dist

            @when(t < T - 1)
            def _():
                add_arrived(d, c)

            slot = jnp.where(dist == 1, T, d)
            sum_copy(d, slot, c, 0).start()

    def last(c):
        @when(t > 0)
        def _():
            sum_wait(t, c)

        @when(t < T - 1)
        def _():
            sum_wait(T, c)

        total = part[t, chunk(c), :].astype(jnp.float32)
        left = rb[t, chunk(c), :].astype(jnp.float32)
        right = rb[T, chunk(c), :].astype(jnp.float32)
        total = total + jnp.where(t > 0, left, 0.0) + jnp.where(t < T - 1, right, 0.0)
        out_ref[chunk(c), :] = total.astype(jnp.bfloat16)

    def own_sends(c):
        gather_send(t, c, 0, own=True)
        gather_send(t, c, 1, own=True)

    own_sends(0)
    for copy in loads:
        copy.wait()

    for c in range(C):
        @pl.loop(1, T)
        def _(dist):
            if c > 0:
                sum_step(T - dist, c - 1)

            @when(dist > 1)
            def _():
                feature_step(dist - 1, c)

            gather_step(dist, c)
            if c == 0:
                @when(dist == 1)
                def _():
                    for k in range(C):
                        low_rank(t, k)

            if c + 1 < C:
                @when(dist == max(T - 2, 1))
                def _():
                    own_sends(c + 1)

            @when(dist > 1)
            def _():
                project_step(dist - 1, c)

        feature_step(T - 1, c)
        project_step(T - 1, c)

    @pl.loop(1, T)
    def _(dist):
        sum_step(T - dist, C - 1)

        @when(dist == 1)
        def _():
            for c in range(C):
                project(t, c)

    for c in range(C):
        last(c)

    @pl.loop(0, T)
    def _(d):
        for c in range(C):
            @when(jnp.logical_and(d >= t, t > 0))
            def _():
                gather_copy(d, c, 0).wait_send()

            @when(jnp.logical_and(d <= t, t < T - 1))
            def _():
                gather_copy(d, c, 1).wait_send()

            @pl.loop(1, Q)
            def _(off):
                rank_copy(d, c, off).wait_send()

            @when(d != t)
            def _():
                sum_copy(d, d, c, 1).wait_send()

                @when(is_root)
                def _():
                    for k in range(1, A):
                        spread_copy(d, c, k - 1, hq, column_target(k)).wait_send()

                @when(in_column)
                def _():
                    for k in range(1, S):
                        spread_copy(d, c, A - 2 + k, ht, sibling_target(k)).wait_send()


def row_codes(adapter_storage_slot, request_adapter, steps):
    catalog = adapter_storage_slot.shape[0]
    matches = request_adapter[:, None] == jnp.arange(catalog, dtype=jnp.int32)[None, :]
    storage = jnp.sum(jnp.where(matches, adapter_storage_slot[None, :], 0), axis=1)
    local_slot = storage - lax.axis_index("tensor") * ADP_HOLD
    return jnp.repeat(local_slot, steps)


def local(
    hidden,
    output_weight,
    adapter_down_weight,
    adapter_up_weight,
    adapter_storage_slot,
    request_adapter,
):
    row_dev, steps, _ = hidden.shape
    T = lax.axis_size("tensor")
    A = lax.axis_size("adapter")
    S = lax.axis_size("sub")
    Q = A * S
    C = CHUNKS
    t = lax.axis_index("tensor")
    q = lax.axis_index(("adapter", "sub"))
    K, N = output_weight.shape
    KQ, X = adapter_down_weight.shape
    assert T == Q and K == KQ
    R = row_dev * steps
    hq = lax.dynamic_slice_in_dim(hidden, q * KQ, KQ, 2).reshape(R, KQ)
    ht = lax.dynamic_slice_in_dim(hidden, t * K, K, 2).reshape(R, K)
    codes = row_codes(adapter_storage_slot, request_adapter, steps).reshape(T, R, 1)
    codes = jnp.broadcast_to(codes, (T, R, LANES))
    bf = jnp.bfloat16
    dma = pltpu.SemaphoreType.DMA
    vmem = pl.BlockSpec(memory_space=pltpu.VMEM)
    anywhere = pl.BlockSpec(memory_space=pl.ANY)
    out = pl.pallas_call(
        functools.partial(kernel, T, A, S, C),
        out_shape=jax.ShapeDtypeStruct((R, N), bf),
        in_specs=[anywhere] * 5 + [vmem],
        out_specs=vmem,
        scratch_shapes=[
            pltpu.VMEM((T, R, KQ), bf),
            pltpu.VMEM((T, R, K), bf),
            pltpu.VMEM((K, N), bf),
            pltpu.VMEM((KQ, X), bf),
            pltpu.VMEM((X, N), bf),
            pltpu.VMEM((Q, T, R, LANES), bf),
            pltpu.VMEM((R // C, X), bf),
            pltpu.VMEM((R // C, N), jnp.float32),
            pltpu.VMEM((T, R, N), bf),
            pltpu.VMEM((T + 1, R, N), bf),
            dma((5,)),
            dma((T, C)),
            dma((2, T, C)),
            dma((T, C)),
            dma((A + S - 2, T, C)),
            dma((T, C)),
            dma((Q, T, C)),
            dma((Q, T, C)),
            dma((T, C)),
            dma((T + 1, C)),
        ],
        compiler_params=pltpu.CompilerParams(
            collective_id=0, has_side_effects=True, vmem_limit_bytes=56 * 1024 * 1024
        ),
        cost_estimate=pl.CostEstimate(
            flops=2 * T * R * (K * N + KQ * X + X * N),
            bytes_accessed=2 * (K * N + KQ * X + X * N + 4 * T * R * K),
            transcendentals=0,
        ),
    )(hq, ht, output_weight, adapter_down_weight, adapter_up_weight, codes)
    return out.reshape(row_dev, steps, N)


def solution(mesh):
    return jax.shard_map(
        local,
        mesh=mesh,
        in_specs=(
            P(("groups", "tensor"), None, None),
            P("tensor", ("adapter", "sub")),
            P(("adapter", "sub"), "tensor"),
            P("tensor", ("adapter", "sub")),
            P("groups"),
            P("groups"),
        ),
        out_specs=P(("groups", "tensor"), None, ("adapter", "sub")),
        check_vma=False,
    )
```
